32 devices in a mesh: seq: 16 (over z, y, x), trk: 2 (over core).
Axes of the slice: x: 2, y: 2, z: 4, core: 2. Of those that a mesh axis runs over, the one named last changes fastest.
Arguments:
- embeddings: bfloat16 [4, 2048, 1920], P(None, 'seq', 'trk'), may hold values from -6 to 6
- head: bfloat16 [1920, 4096], P(None, 'trk'), may hold values from -0.125 to 0.125
- exon_starts: int32 [4, 32, 8], replicated, may hold values from 0 to 2040, as said below
- exon_lengths: int32 [4, 32, 8], replicated, may hold values from 1 to 8, as said below
- gene_owner: int32 [4, 32], replicated, may hold values from 0 to 15, as said below
- gene_targets: float32 [4, 64, 4096], P(None, 'seq', 'trk'), may hold values from 2 to 400, as said below
Outputs:
- gene_pred: float32 [4, 64, 4096], P(None, 'seq', 'trk')
- loss: float32 [4, 4096], P(None, 'trk')
- grad_head: float32 [1920, 4096], P('seq', 'trk')
The draws below stay inside these ranges and needn't reach their ends.
Inputs may be any that keep to these rules, and one draw needn't show every extreme that they name: `exon_starts`: each gene has 8 exon blocks; blocks may intersect. Some block of each window starts at 0 and some at 2040. `exon_lengths`: some block of each window has length 8. `gene_owner`: in each window no owner holds more than 4 genes, and some owner holds exactly 4. `gene_targets`: entries of empty slots are read by nothing.
All inputs are finite; a program needn't handle non-finite values.
Results may differ from the reference program's by a relative error of at most 0.0041.
Values may be sent and summed in bfloat16 or wider, within the bound.
A program may use at most 128 MiB of HBM per device.

```python
import jax
import jax.numpy as jnp
from jax import lax

D = 1920
TRACKS = 4096
WINDOWS = 4
CAP = 4
EXONS = 8
EXON_MAX = 8
BINS = 2048
GENES = 32
SLOTS = 64


def draw_exon_starts(key, part):
    first_key, second_key = jax.random.split(jax.random.fold_in(key, 11))
    reach = BINS // 4
    upper = BINS - EXON_MAX
    anchor = jax.random.randint(first_key, (WINDOWS, GENES, 1), 0, upper - reach + 1)
    offset = jax.random.randint(second_key, (WINDOWS, GENES, EXONS), 0, reach + 1)
    starts = anchor + offset
    starts = starts.at[:, 0, 0].set(0)
    starts = starts.at[:, 0, 1].set(upper)
    return starts.astype(jnp.int32)


def draw_exon_lengths(key, part):
    lengths = jax.random.randint(jax.random.fold_in(key, 23), (WINDOWS, GENES, EXONS), 1, EXON_MAX + 1)
    lengths = lengths.at[:, 0, 0].set(EXON_MAX)
    return lengths.astype(jnp.int32)


def draw_gene_owner(key, part):
    window_keys = jax.random.split(jax.random.fold_in(key, 37), WINDOWS)
    owners_total = SLOTS // CAP

    def single(window_key):
        pick_key, perm_key, order_key = jax.random.split(window_key, 3)
        busiest = jax.random.randint(pick_key, (), 0, owners_total)
        slot_owner = jax.random.permutation(perm_key, SLOTS) // CAP
        ordering = jnp.argsort((slot_owner == busiest).astype(jnp.int32), stable=True)
        others = slot_owner[ordering][:GENES - CAP].astype(jnp.int32)
        filled = jnp.concatenate([jnp.zeros((CAP,), jnp.int32) + busiest.astype(jnp.int32), others])
        return filled[jax.random.permutation(order_key, GENES)]
    return jax.vmap(single)(window_keys).astype(jnp.int32)


def draw_gene_targets(key, part):
    second_key = jax.random.fold_in(jax.random.fold_in(key, 41), 1)
    shape = (WINDOWS, SLOTS, TRACKS)
    position = jnp.arange(SLOTS, dtype=jnp.float32) / (SLOTS - 1)
    rising = 1.0 + 2.0 * position
    base = jnp.exp(jax.random.uniform(second_key, shape, jnp.float32, jnp.log(2.0), jnp.log(40.0)))
    values = base * rising[None, :, None]
    return values.astype(jnp.float32)


def with_spikes(array, rng, source, target, shards_of, factor):
    def block_of(dim):
        return (jnp.arange(array.shape[dim]) // (array.shape[dim] // shards_of)).reshape((-1,) + (1,) * (array.ndim - 1 - dim))

    near = jax.random.permutation(rng, shards_of)[block_of(target)]
    far = (block_of(target) + shards_of // 2) % shards_of
    return jnp.where((block_of(source) == near) | (block_of(source) == far), factor * array, array)


def levels(key, extent, pieces, smallest, top_value):
    loudness, own = 1.0, jax.random.fold_in(key, 6)
    for dim, parts in pieces:
        draws = jnp.exp(jax.random.uniform(jax.random.fold_in(own, dim), (parts,), jnp.float32, smallest / len(pieces), top_value / len(pieces)))
        loudness = loudness * jnp.repeat(draws, extent[dim] // parts).reshape([-1 if axis == dim else 1 for axis in range(len(extent))])
    return loudness


def noise(rng, dims, scale, most, cuts=(), held_as=jnp.bfloat16):
    result = jax.random.normal(rng, dims, jnp.float32) * scale
    if len(cuts) > 0:
        result = levels(rng, dims, cuts, -0.22, 0.18) * result
    return jnp.clip(result, min=-most, max=most).astype(held_as)


def bell_draw_with(stream_key, shape, scale, bound, shards, heavy, kind=jnp.bfloat16):
    values = scale * jax.random.normal(stream_key, shape, jnp.float32)
    if shards:
        values = values * levels(stream_key, shape, shards, -0.22, 0.18)
    return jnp.clip(with_spikes(values, jax.random.fold_in(stream_key, 3), *heavy), -bound, bound).astype(kind)


def setup_inputs(seed: int = 0) -> dict:
    seeds = jax.random.split(jax.random.key(seed), 7)
    return {
        "embeddings": bell_draw_with(seeds[0], (WINDOWS, BINS, D), 1.0, 6.0, ((1, 16), (2, 2)), (1, 2, 16, 2.0)),
        "head": noise(seeds[1], (D, TRACKS), D ** -0.5, 0.125, ((1, 2),)),
        "exon_starts": draw_exon_starts(jax.random.fold_in(seeds[6], 71), 0),
        "exon_lengths": draw_exon_lengths(jax.random.fold_in(seeds[6], 71), 0),
        "gene_owner": draw_gene_owner(jax.random.fold_in(seeds[6], 71), 0),
        "gene_targets": draw_gene_targets(jax.random.fold_in(seeds[6], 71), 0),
    }


def slot_table(gene_owner, capacity):
    genes = gene_owner.shape[1]
    same = gene_owner[:, :, None] == gene_owner[:, None, :]
    earlier = jnp.arange(genes)[None, :] < jnp.arange(genes)[:, None]
    ahead = jnp.sum((same & earlier[None]).astype(jnp.int32), axis=2)
    return (gene_owner * capacity + ahead).astype(jnp.int32)


def coverage(starts, lengths, positions):
    where_bin = positions[None, None, None, :]
    inside = (where_bin >= starts[..., None]) & (where_bin < (starts + lengths)[..., None])
    return jnp.sum(inside.astype(jnp.float32), axis=2)


def reference(embeddings, head, exon_starts, exon_lengths, gene_owner, gene_targets):
    slot_of = slot_table(gene_owner, CAP)
    onehot = (slot_of[..., None] == jnp.arange(SLOTS, dtype=jnp.int32)).astype(jnp.float32)
    valid = jnp.sum(onehot, axis=1)
    cover = coverage(exon_starts, exon_lengths, jnp.arange(BINS, dtype=jnp.int32))
    member = jnp.einsum("wgs,wgb->wsb", onehot, cover, precision=lax.Precision.HIGHEST).astype(jnp.bfloat16)

    def forward(pair):
        rows, members = pair
        pred = jax.nn.softplus(jnp.dot(rows, head, preferred_element_type=jnp.float32)).astype(jnp.bfloat16)
        return jnp.dot(members, pred, preferred_element_type=jnp.float32)

    gene_pred = lax.map(forward, (embeddings, member))
    targets = gene_targets * valid[..., None]
    total = jnp.sum(gene_pred, axis=1)
    target_sum = jnp.sum(targets, axis=1)
    safe = jnp.where(valid[..., None] > 0, gene_pred, 1.0)
    fit = jnp.sum(targets * jnp.log(safe), axis=1)
    log_total = jnp.log(total)
    loss = (-fit + target_sum * log_total + 0.2 * (total - target_sum * log_total)) / target_sum
    scale_rows = (GENES / target_sum)[:, None, :]
    gene_grad = (scale_rows * (valid[..., None] * (0.2 + 0.8 * target_sum / total)[:, None, :] - targets / safe)).astype(jnp.bfloat16)

    def backward(carry, triple):
        rows, members, grads = triple
        logits = jnp.dot(rows, head, preferred_element_type=jnp.float32)
        spread = jnp.dot(members.T, grads, preferred_element_type=jnp.float32)
        logit_grad = (spread * jax.nn.sigmoid(logits)).astype(jnp.bfloat16)
        return carry + jnp.dot(rows.T, logit_grad, preferred_element_type=jnp.float32), None

    grad_head, _ = lax.scan(backward, jnp.zeros((D, TRACKS), jnp.float32), (embeddings, member, gene_grad))
    return gene_pred, loss, grad_head
```

```python
import functools

import jax
import jax.numpy as jnp
from jax import lax
from jax.experimental import pallas as pl
from jax.experimental.pallas import tpu as pltpu
from jax.sharding import PartitionSpec as P

MESH = pl.DeviceIdType.MESH
HIGHEST = lax.Precision.HIGHEST


def slot_table(gene_owner, capacity):
    genes = gene_owner.shape[1]
    same = gene_owner[:, :, None] == gene_owner[:, None, :]
    earlier = jnp.arange(genes)[None, :] < jnp.arange(genes)[:, None]
    ahead = jnp.sum((same & earlier[None]).astype(jnp.int32), axis=2)
    return gene_owner * capacity + ahead


def coverage(starts, lengths, positions):
    where_bin = positions[None, None, None, :]
    inside = (where_bin >= starts[..., None]) & (where_bin < (starts + lengths)[..., None])
    return jnp.sum(inside.astype(jnp.float32), axis=2)


def kernel(
    dims,
    x_ref, head_ref, mem_ref, pick_ref, give_ref, tgt_ref,
    grad_ref, gene_ref, loss_ref,
    x_all, pred, sig, part, part_in, grads, tgt_in, gene_out, loss_out, lgrad, acc, block_out, block_in,
    near_send, near_recv, sib_send, sib_recv, tgt_send, tgt_recv, part_send, part_recv,
    grads_send, grads_recv, gene_send, gene_recv, loss_send, loss_recv, block_send, block_recv,
):
    n_seq, n_trk, windows, group, genes, own_rows = dims
    me = lax.axis_index("seq")
    core = lax.axis_index("trk")
    win = me // group
    place = lax.rem(me, group)
    rows = x_ref.shape[0]
    chans = x_ref.shape[1]
    tracks = head_ref.shape[2]
    tile = 256 if rows % 256 == 0 else rows

    def to_seq(src, dst, send, recv, there):
        return pltpu.make_async_remote_copy(
            src_ref=src, dst_ref=dst, send_sem=send, recv_sem=recv,
            device_id={"seq": there}, device_id_type=MESH,
        )

    def to_core(src, dst, send, recv, there):
        return pltpu.make_async_remote_copy(
            src_ref=src, dst_ref=dst, send_sem=send, recv_sem=recv,
            device_id={"trk": there}, device_id_type=MESH,
        )

    barrier = pltpu.get_barrier_semaphore()

    @pl.loop(1, n_seq)
    def _(k):
        pl.semaphore_signal(
            barrier, inc=1, device_id={"seq": lax.rem(me + k, n_seq)}, device_id_type=MESH
        )

    for k in range(1, n_trk):
        pl.semaphore_signal(
            barrier, inc=1, device_id={"trk": lax.rem(core + k, n_trk)}, device_id_type=MESH
        )
    pl.semaphore_wait(barrier, n_seq - 1 + n_trk - 1)

    def near(k):
        there = lax.rem(place + k, group)
        return to_seq(
            x_ref, x_all.at[core, place], near_send.at[there], near_recv.at[place],
            win * group + there,
        )

    def near_arrival(k):
        frm = lax.rem(place + k, group)
        return to_seq(
            x_ref, x_all.at[core, frm], near_send.at[frm], near_recv.at[frm], win * group + frm
        )

    def sibling(k, source, slot):
        there = lax.rem(core + k, n_trk)
        return to_core(
            source, x_all.at[core, slot], sib_send.at[there, slot], sib_recv.at[core, slot], there
        )

    def sibling_arrival(k, slot):
        frm = lax.rem(core + k, n_trk)
        return to_core(
            x_ref, x_all.at[frm, slot], sib_send.at[frm, slot], sib_recv.at[frm, slot], frm
        )

    for k in range(1, group):
        near(k).start()
    for k in range(1, n_trk):
        sibling(k, x_ref, place).start()
    x_all[core, place] = x_ref[...]

    def tgt_copy(k):
        there = lax.rem(me + k, n_seq)
        return to_seq(tgt_ref.at[there], tgt_in.at[me], tgt_send.at[there], tgt_recv.at[me], there)

    @pl.loop(1, n_seq)
    def _(k):
        tgt_copy(k).start()

    tgt_in[me] = tgt_ref[me]

    part[...] = jnp.zeros_like(part)

    def forward(slot):
        @pl.loop(0, rows // tile)
        def _(i):
            at = pl.ds(pl.multiple_of(i * tile, tile), tile)
            logits = jnp.dot(
                x_all[0, slot, at, :], head_ref[0], preferred_element_type=jnp.float32
            )
            for c in range(1, n_trk):
                logits += jnp.dot(
                    x_all[c, slot, at, :], head_ref[c], preferred_element_type=jnp.float32
                )
            small = jnp.exp(-jnp.abs(logits))
            pred[at, :] = (jnp.maximum(logits, 0.0) + jnp.log1p(small)).astype(jnp.bfloat16)
            sig[slot, at, :] = jnp.where(logits >= 0, 1.0, small) / (1.0 + small)

        part[...] += jnp.dot(
            mem_ref[slot], pred[...], preferred_element_type=jnp.float32
        ).reshape(part.shape)

    for k in range(1, group + 1):
        if k < group:
            near_arrival(k).wait_recv()
            frm = lax.rem(place + k, group)
            for j in range(1, n_trk):
                sibling(j, x_all.at[core, frm], frm).start()
        slot = lax.rem(place + k - 1, group)
        for j in range(1, n_trk):
            sibling_arrival(j, slot).wait_recv()
        forward(slot)

    def part_copy(k):
        there = lax.rem(win + k, windows)
        return to_seq(
            part.at[there], part_in.at[win], part_send.at[there], part_recv.at[win],
            there * group + place,
        )

    for k in range(1, windows):
        part_copy(k).start()

    @pl.loop(1, n_seq)
    def _(k):
        frm = lax.rem(me + k, n_seq)
        to_seq(
            tgt_ref.at[frm], tgt_in.at[frm], tgt_send.at[frm], tgt_recv.at[frm], frm
        ).wait_recv()

    tgt = jnp.dot(
        pick_ref[...], tgt_in[...].reshape(-1, tracks),
        preferred_element_type=jnp.float32, precision=HIGHEST,
    )
    tsum = jnp.sum(tgt, axis=0, keepdims=True)
    part_in[win] = part[win]
    for k in range(1, windows):
        frm = lax.rem(win + k, windows)
        to_seq(
            part.at[frm], part_in.at[frm], part_send.at[frm], part_recv.at[frm],
            frm * group + place,
        ).wait_recv()
    gene = part_in[0]
    for k in range(1, windows):
        gene += part_in[k]
    total = jnp.sum(gene, axis=0, keepdims=True)
    grads[win] = (
        (genes / tsum) * ((0.2 + 0.8 * tsum / total) - tgt / gene)
    ).astype(jnp.bfloat16)

    def grads_copy(k):
        there = lax.rem(win + k, windows)
        return to_seq(
            grads.at[win], grads.at[win], grads_send.at[there], grads_recv.at[win],
            there * group + place,
        )

    for k in range(1, windows):
        grads_copy(k).start()

    fit = jnp.sum(tgt * jnp.log(gene), axis=0, keepdims=True)
    log_total = jnp.log(total)
    loss = (-fit + tsum * log_total + 0.2 * (total - tsum * log_total)) / tsum
    loss_out[...] = jnp.broadcast_to(loss, loss_out.shape)
    gene_out[...] = jnp.dot(
        give_ref[...], gene, preferred_element_type=jnp.float32, precision=HIGHEST
    ).reshape(gene_out.shape)

    def gene_copy(k):
        there = lax.rem(me + k, n_seq)
        return to_seq(
            gene_out.at[there], gene_ref.at[me], gene_send.at[there], gene_recv.at[me], there
        )

    def loss_copy(k):
        there = lax.rem(me + k, n_seq)
        return to_seq(loss_out, loss_ref.at[me], loss_send.at[there], loss_recv.at[me], there)

    gene_ref[me] = gene_out[me]
    loss_ref[me] = loss_out[...]

    for k in range(1, windows):
        frm = lax.rem(win + k, windows)
        to_seq(
            grads.at[frm], grads.at[frm], grads_send.at[frm], grads_recv.at[frm],
            frm * group + place,
        ).wait_recv()

    @pl.loop(1, n_seq)
    def _(k):
        gene_copy(k).start()
        loss_copy(k).start()

    @pl.loop(0, group)
    def _(slot):
        spread = lax.dot_general(
            mem_ref[slot], grads[...].reshape(-1, tracks), (((0,), (0,)), ((), ())),
            preferred_element_type=jnp.float32,
        )
        lgrad[slot] = (spread * sig[slot]).astype(jnp.bfloat16)

    blocks = n_seq // n_trk

    def block_copy(there):
        return to_seq(
            block_out.at[there], block_in.at[me], block_send.at[there], block_recv.at[me], there
        )

    for c in range(n_trk):
        acc[...] = jnp.zeros_like(acc)

        @pl.loop(0, group)
        def _(slot):
            acc[...] += lax.dot_general(
                x_all[c, slot], lgrad[slot], (((0,), (0,)), ((), ())),
                preferred_element_type=jnp.float32,
            )

        for j in range(blocks):
            there = c * blocks + j
            value = acc[j * own_rows:(j + 1) * own_rows].astype(jnp.bfloat16)
            spare = block_out.shape[1] - own_rows
            if spare:
                value = jnp.concatenate([value, jnp.zeros((spare, tracks), jnp.bfloat16)], axis=0)
            block_out[there] = value

            @pl.when(me != there)
            def _():
                block_copy(there).start()

    block_in[me] = block_out[me]

    @pl.loop(1, n_seq)
    def _(k):
        frm = lax.rem(me + k, n_seq)
        to_seq(
            block_out.at[frm], block_in.at[frm], block_send.at[frm], block_recv.at[frm], frm
        ).wait_recv()

    for p in range(group):
        whole = block_in[p].astype(jnp.float32)
        for w in range(1, windows):
            whole += block_in[w * group + p].astype(jnp.float32)
        grad_ref[p] = whole

    @pl.loop(1, n_seq)
    def _(k):
        frm = lax.rem(me + k, n_seq)
        to_seq(
            gene_out.at[frm], gene_ref.at[frm], gene_send.at[frm], gene_recv.at[frm], frm
        ).wait_recv()
        to_seq(loss_out, loss_ref.at[frm], loss_send.at[frm], loss_recv.at[frm], frm).wait_recv()
        tgt_copy(k).wait_send()
        gene_copy(k).wait_send()
        loss_copy(k).wait_send()
        block_copy(frm).wait_send()

    for k in range(1, windows):
        part_copy(k).wait_send()
        grads_copy(k).wait_send()
    for k in range(1, group):
        near(k).wait_send()
    for k in range(1, n_trk):
        sibling(k, x_ref, place).wait_send()
        for j in range(1, group):
            frm = lax.rem(place + j, group)
            sibling(k, x_all.at[core, frm], frm).wait_send()


def round_up(n, m):
    return (n + m - 1) // m * m


def per_device(embeddings, head, exon_starts, exon_lengths, gene_owner, gene_targets):
    n_seq = lax.axis_size("seq")
    n_trk = lax.axis_size("trk")
    me = lax.axis_index("seq")
    windows, bin_dev, chans = embeddings.shape
    genes = gene_owner.shape[1]
    capacity = gene_targets.shape[1]
    group = n_seq // windows
    win, place = me // group, me % group
    depth, track_dev = head.shape
    tracks = track_dev // group
    rows = windows * bin_dev
    own_rows = depth // n_seq
    row_pad = round_up(own_rows, 16)
    cap_pad = round_up(capacity, 8)
    bf16, f32 = jnp.bfloat16, jnp.float32

    positions = win * group * bin_dev + jnp.arange(group * bin_dev, dtype=jnp.int32)
    cover = coverage(exon_starts, exon_lengths, positions).reshape(windows, genes, group, bin_dev)
    same = jnp.eye(windows, dtype=f32)
    mem = cover.transpose(2, 0, 1, 3)[:, :, :, None, :] * same[None, :, None, :, None]
    mem = mem.reshape(group, windows * genes, rows).astype(bf16)
    slot_here = lax.dynamic_index_in_dim(slot_table(gene_owner, capacity), win, 0, keepdims=False)
    padded = slot_here // capacity * cap_pad + slot_here % capacity
    every = jnp.arange(n_seq * cap_pad, dtype=jnp.int32)
    pick = (padded[:, None] == every[None, :]).astype(f32)
    give = (padded[None, :] == every[:, None]).astype(f32)
    head_here = lax.dynamic_slice_in_dim(head, place * tracks, tracks, 1).reshape(
        n_trk, chans, tracks
    )
    tgt = gene_targets.reshape(windows, capacity, group, tracks).transpose(0, 2, 1, 3)
    tgt = jnp.pad(
        tgt.reshape(n_seq, capacity, tracks), ((0, 0), (0, cap_pad - capacity), (0, 0))
    )

    dma = pltpu.SemaphoreType.DMA
    vmem = pl.BlockSpec(memory_space=pltpu.VMEM)
    grad, gene, loss = pl.pallas_call(
        functools.partial(kernel, (n_seq, n_trk, windows, group, genes, own_rows)),
        out_shape=(
            jax.ShapeDtypeStruct((group, row_pad, tracks), f32),
            jax.ShapeDtypeStruct((n_seq, cap_pad, tracks), f32),
            jax.ShapeDtypeStruct((n_seq, 8, tracks), f32),
        ),
        in_specs=[vmem] * 6,
        out_specs=(vmem, vmem, vmem),
        scratch_shapes=[
            pltpu.VMEM((n_trk, group, rows, chans), bf16),
            pltpu.VMEM((rows, tracks), bf16),
            pltpu.VMEM((group, rows, tracks), f32),
            pltpu.VMEM((windows, genes, tracks), f32),
            pltpu.VMEM((windows, genes, tracks), f32),
            pltpu.VMEM((windows, genes, tracks), bf16),
            pltpu.VMEM((n_seq, cap_pad, tracks), f32),
            pltpu.VMEM((n_seq, cap_pad, tracks), f32),
            pltpu.VMEM((8, tracks), f32),
            pltpu.VMEM((group, rows, tracks), bf16),
            pltpu.VMEM((chans, tracks), f32),
            pltpu.VMEM((n_seq, row_pad, tracks), bf16),
            pltpu.VMEM((n_seq, row_pad, tracks), bf16),
            dma((group,)), dma((group,)),
            dma((n_trk, group)), dma((n_trk, group)),
            dma((n_seq,)), dma((n_seq,)),
            dma((windows,)), dma((windows,)),
            dma((windows,)), dma((windows,)),
            dma((n_seq,)), dma((n_seq,)),
            dma((n_seq,)), dma((n_seq,)),
            dma((n_seq,)), dma((n_seq,)),
        ],
        compiler_params=pltpu.CompilerParams(
            collective_id=0, has_side_effects=True, vmem_limit_bytes=60 * 1024 * 1024
        ),
    )(embeddings.reshape(rows, chans), head_here, mem, pick, give, tgt)

    grad_head = grad[:, :own_rows].transpose(1, 0, 2).reshape(own_rows, track_dev)
    gene_here = gene[:, :capacity].reshape(windows, group, capacity, tracks)
    gene_here = gene_here.transpose(0, 2, 1, 3).reshape(windows, capacity, track_dev)
    return gene_here, loss[:, 0].reshape(windows, track_dev), grad_head


def solution(mesh):
    return jax.shard_map(
        per_device,
        mesh=mesh,
        in_specs=(P(None, "seq", "trk"), P(None, "trk"), P(), P(), P(), P(None, "seq", "trk")),
        out_specs=(P(None, "seq", "trk"), P(None, "trk"), P("seq", "trk")),
        check_vma=False,
    )
```

```python
import functools

import jax
import jax.numpy as jnp
from jax import lax
from jax.experimental import pallas as pl
from jax.experimental.pallas import tpu as pltpu
from jax.sharding import PartitionSpec as P

MESH = pl.DeviceIdType.MESH
HIGHEST = lax.Precision.HIGHEST


def kernel(
    dims,
    x_hbm, head_hbm, starts_ref, lengths_ref, owner_ref, targets_ref,
    grad_ref, gene_ref, loss_ref,
    x_all, head_ref, mem_ref, tgt_ref, gene_in, loss_in, pred, sig, part, part_in, grads, tgt_in, gene_out, loss_out, lgrad, acc, block_out, block_in,
    near_send, near_recv, sib_send, sib_recv, tgt_send, tgt_recv, part_send, part_recv,
    grads_send, grads_recv, gene_send, gene_recv, loss_send, loss_recv, block_send, block_recv,
    diag_send, diag_recv, own_sem, head_sem,
):
    n_seq, n_trk, windows, group, genes, own_rows = dims
    me = lax.axis_index("seq")
    core = lax.axis_index("trk")
    win = me // group
    place = lax.rem(me, group)
    rows, chans = x_all.shape[2:]
    tracks = head_ref.shape[2]
    bin_dev = rows // windows
    capacity = targets_ref.shape[1]
    cap_pad = tgt_ref.shape[1]
    square = group == 4 and rows % 32 == 0
    tile = 256 if rows % 256 == 0 else rows

    def to_seq(src, dst, send, recv, there):
        return pltpu.make_async_remote_copy(
            src_ref=src, dst_ref=dst, send_sem=send, recv_sem=recv,
            device_id={"seq": there}, device_id_type=MESH,
        )

    def to_core(src, dst, send, recv, there):
        return pltpu.make_async_remote_copy(
            src_ref=src, dst_ref=dst, send_sem=send, recv_sem=recv,
            device_id={"trk": there}, device_id_type=MESH,
        )

    barrier = pltpu.get_barrier_semaphore()

    @pl.loop(1, n_seq)
    def _(k):
        pl.semaphore_signal(
            barrier, inc=1, device_id={"seq": lax.rem(me + k, n_seq)}, device_id_type=MESH
        )

    for k in range(1, n_trk):
        pl.semaphore_signal(
            barrier, inc=1, device_id={"trk": lax.rem(core + k, n_trk)}, device_id_type=MESH
        )
    pl.semaphore_wait(barrier, n_seq - 1 + n_trk - 1)

    def near_to(there):
        return to_seq(
            x_hbm, x_all.at[core, place], near_send.at[there], near_recv.at[place],
            win * group + there,
        )

    def near_from(frm):
        return to_seq(
            x_hbm, x_all.at[core, frm], near_send.at[frm], near_recv.at[frm], win * group + frm
        )

    def sibling(k, source, slot):
        there = lax.rem(core + k, n_trk)
        return to_core(
            source, x_all.at[core, slot], sib_send.at[there, slot], sib_recv.at[core, slot], there
        )

    def sibling_arrival(k, slot):
        frm = lax.rem(core + k, n_trk)
        return to_core(
            x_hbm, x_all.at[frm, slot], sib_send.at[frm, slot], sib_recv.at[frm, slot], frm
        )

    half = rows // 2
    beside = place + 1 - 2 * lax.rem(place, 2)
    across = lax.rem(place + 2, group)
    corner = group - 1 - place

    def pass_on(part_of, frm, there):
        at = x_all.at[core, frm, pl.ds(part_of * half, half)]
        return to_seq(
            at, at, diag_send.at[part_of], diag_recv.at[part_of], win * group + there
        )

    if square:
        order = [beside, across, corner]
        near_to(beside).start()
        near_to(across).start()
    else:
        order = [lax.rem(place + k, group) for k in range(1, group)]
        for there in order:
            near_to(there).start()
    for k in range(1, n_trk):
        sibling(k, x_hbm, place).start()
    own_copy = pltpu.make_async_copy(x_hbm, x_all.at[core, place], own_sem)
    own_copy.start()
    if head_hbm.shape[2] == tracks:
        head_copy = pltpu.make_async_copy(head_hbm, head_ref, head_sem)
    else:
        at = pl.ds(pl.multiple_of(place * tracks, tracks), tracks)
        head_copy = pltpu.make_async_copy(head_hbm.at[:, :, at], head_ref, head_sem)
    head_copy.start()

    def tgt_copy(k):
        there = lax.rem(me + k, n_seq)
        return to_seq(tgt_ref.at[there], tgt_in.at[me], tgt_send.at[there], tgt_recv.at[me], there)

    tgt_ref[...] = jnp.zeros_like(tgt_ref)
    for w in range(windows):
        for p in range(group):
            tgt_ref[w * group + p, :capacity, :] = (
                targets_ref[w, :, p * tracks:(p + 1) * tracks]
            )

    @pl.loop(1, n_seq)
    def _(k):
        tgt_copy(k).start()

    tgt_in[me] = tgt_ref[me]

    mem_ref[...] = jnp.zeros_like(mem_ref)
    exons = starts_ref.shape[2]

    @pl.loop(0, group)
    def _(slot):
        bins = (win * group + slot) * bin_dev + lax.broadcasted_iota(
            jnp.int32, (genes, bin_dev), 1
        )
        for w in range(windows):
            first, extent = starts_ref[w], lengths_ref[w]
            count = jnp.zeros((genes, bin_dev), jnp.float32)
            for e in range(exons):
                begin = first[:, e:e + 1]
                end = begin + extent[:, e:e + 1]
                count += jnp.where((bins >= begin) & (bins < end), 1.0, 0.0)
            mem_ref[slot, w * genes:(w + 1) * genes, w * bin_dev:(w + 1) * bin_dev] = (
                count.astype(jnp.bfloat16)
            )

    owner_row = owner_ref[pl.ds(win, 1), :]
    down = lax.broadcasted_iota(jnp.int32, (genes, genes), 0)
    along = lax.broadcasted_iota(jnp.int32, (genes, genes), 1)
    spread_row = jnp.broadcast_to(owner_row, (genes, genes))
    owner_col = jnp.sum(jnp.where(down == along, spread_row, 0), axis=1, keepdims=True)
    same = spread_row == owner_col
    rank_col = jnp.sum(jnp.where(same & (along < down), 1, 0), axis=1, keepdims=True)
    rank_row = jnp.sum(jnp.where(same & (down < along), 1, 0), axis=0, keepdims=True)
    slot_col = owner_col * cap_pad + rank_col
    slot_row = owner_row * cap_pad + rank_row
    slots = n_seq * cap_pad
    pick = jnp.where(
        slot_col == lax.broadcasted_iota(jnp.int32, (genes, slots), 1), 1.0, 0.0
    )
    give = jnp.where(
        slot_row == lax.broadcasted_iota(jnp.int32, (slots, genes), 0), 1.0, 0.0
    )

    part[...] = jnp.zeros_like(part)

    def forward(slot):
        @pl.loop(0, rows // tile)
        def _(i):
            at = pl.ds(pl.multiple_of(i * tile, tile), tile)
            logits = jnp.dot(
                x_all[0, slot, at, :], head_ref[0], preferred_element_type=jnp.float32
            )
            for c in range(1, n_trk):
                logits += jnp.dot(
                    x_all[c, slot, at, :], head_ref[c], preferred_element_type=jnp.float32
                )
            small = jnp.exp(-jnp.abs(logits))
            pred[at, :] = (jnp.maximum(logits, 0.0) + jnp.log1p(small)).astype(jnp.bfloat16)
            sig[slot, at, :] = jnp.where(logits >= 0, 1.0, small) / (1.0 + small)

        part[...] += jnp.dot(
            mem_ref[slot], pred[...], preferred_element_type=jnp.float32
        ).reshape(part.shape)

    own_copy.wait()
    head_copy.wait()

    def hand_over(frm):
        for j in range(1, n_trk):
            sibling(j, x_all.at[core, frm], frm).start()

    if square:
        near_from(beside).wait_recv()
        pass_on(0, beside, across).start()
        hand_over(beside)
        near_from(across).wait_recv()
        pass_on(1, across, beside).start()
        hand_over(across)
        ready = [place, beside, across]
    else:
        ready = [place]
    for slot in ready:
        for j in range(1, n_trk):
            sibling_arrival(j, slot).wait_recv()
        forward(slot)
    for frm in order[len(ready) - 1:]:
        if square:
            pass_on(0, frm, across).wait_recv()
            pass_on(1, frm, beside).wait_recv()
        else:
            near_from(frm).wait_recv()
        hand_over(frm)
        for j in range(1, n_trk):
            sibling_arrival(j, frm).wait_recv()
        forward(frm)

    def part_copy(k):
        there = lax.rem(win + k, windows)
        return to_seq(
            part.at[there], part_in.at[win], part_send.at[there], part_recv.at[win],
            there * group + place,
        )

    for k in range(1, windows):
        part_copy(k).start()

    @pl.loop(1, n_seq)
    def _(k):
        frm = lax.rem(me + k, n_seq)
        to_seq(
            tgt_ref.at[frm], tgt_in.at[frm], tgt_send.at[frm], tgt_recv.at[frm], frm
        ).wait_recv()

    tgt = jnp.dot(
        pick, tgt_in[...].reshape(-1, tracks),
        preferred_element_type=jnp.float32, precision=HIGHEST,
    )
    tsum = jnp.sum(tgt, axis=0, keepdims=True)
    part_in[win] = part[win]
    for k in range(1, windows):
        frm = lax.rem(win + k, windows)
        to_seq(
            part.at[frm], part_in.at[frm], part_send.at[frm], part_recv.at[frm],
            frm * group + place,
        ).wait_recv()
    gene = part_in[0]
    for k in range(1, windows):
        gene += part_in[k]
    total = jnp.sum(gene, axis=0, keepdims=True)
    grads[win] = (
        (genes / tsum) * ((0.2 + 0.8 * tsum / total) - tgt / gene)
    ).astype(jnp.bfloat16)

    def grads_copy(k):
        there = lax.rem(win + k, windows)
        return to_seq(
            grads.at[win], grads.at[win], grads_send.at[there], grads_recv.at[win],
            there * group + place,
        )

    for k in range(1, windows):
        grads_copy(k).start()

    fit = jnp.sum(tgt * jnp.log(gene), axis=0, keepdims=True)
    log_total = jnp.log(total)
    loss = (-fit + tsum * log_total + 0.2 * (total - tsum * log_total)) / tsum
    loss_out[...] = jnp.broadcast_to(loss, loss_out.shape)
    gene_out[...] = jnp.dot(
        give, gene, preferred_element_type=jnp.float32, precision=HIGHEST
    ).reshape(gene_out.shape)

    def gene_copy(k):
        there = lax.rem(me + k, n_seq)
        return to_seq(
            gene_out.at[there], gene_in.at[me], gene_send.at[there], gene_recv.at[me], there
        )

    def loss_copy(k):
        there = lax.rem(me + k, n_seq)
        return to_seq(loss_out, loss_in.at[me], loss_send.at[there], loss_recv.at[me], there)

    gene_in[me] = gene_out[me]
    loss_in[me] = loss_out[...]

    for k in range(1, windows):
        frm = lax.rem(win + k, windows)
        to_seq(
            grads.at[frm], grads.at[frm], grads_send.at[frm], grads_recv.at[frm],
            frm * group + place,
        ).wait_recv()

    @pl.loop(1, n_seq)
    def _(k):
        gene_copy(k).start()
        loss_copy(k).start()

    @pl.loop(0, group)
    def _(slot):
        spread = lax.dot_general(
            mem_ref[slot], grads[...].reshape(-1, tracks), (((0,), (0,)), ((), ())),
            preferred_element_type=jnp.float32,
        )
        lgrad[slot] = (spread * sig[slot]).astype(jnp.bfloat16)

    blocks = n_seq // n_trk

    def block_copy(there):
        return to_seq(
            block_out.at[there], block_in.at[me], block_send.at[there], block_recv.at[me], there
        )

    for i in range(n_trk):
        c = lax.rem(2 * n_trk - 1 - win * n_trk // windows + i, n_trk)
        acc[...] = jnp.zeros_like(acc)

        @pl.loop(0, group)
        def _(slot):
            acc[...] += lax.dot_general(
                x_all[c, slot], lgrad[slot], (((0,), (0,)), ((), ())),
                preferred_element_type=jnp.float32,
            )

        for j in range(blocks):
            there = c * blocks + j
            value = acc[j * own_rows:(j + 1) * own_rows].astype(jnp.bfloat16)
            spare = block_out.shape[1] - own_rows
            if spare:
                value = jnp.concatenate([value, jnp.zeros((spare, tracks), jnp.bfloat16)], axis=0)
            block_out[there] = value

            @pl.when(me != there)
            def _():
                block_copy(there).start()

    block_in[me] = block_out[me]

    @pl.loop(1, n_seq)
    def _(k):
        frm = lax.rem(me + k, n_seq)
        to_seq(
            block_out.at[frm], block_in.at[frm], block_send.at[frm], block_recv.at[frm], frm
        ).wait_recv()

    for p in range(group):
        whole = block_in[p].astype(jnp.float32)
        for w in range(1, windows):
            whole += block_in[w * group + p].astype(jnp.float32)
        grad_ref[:, p * tracks:(p + 1) * tracks] = whole[:own_rows]

    @pl.loop(1, n_seq)
    def _(k):
        frm = lax.rem(me + k, n_seq)
        to_seq(
            gene_out.at[frm], gene_in.at[frm], gene_send.at[frm], gene_recv.at[frm], frm
        ).wait_recv()
        to_seq(loss_out, loss_in.at[frm], loss_send.at[frm], loss_recv.at[frm], frm).wait_recv()
        tgt_copy(k).wait_send()
        gene_copy(k).wait_send()
        loss_copy(k).wait_send()
        block_copy(frm).wait_send()

    for k in range(1, windows):
        part_copy(k).wait_send()
        grads_copy(k).wait_send()
    for w in range(windows):
        for p in range(group):
            at = slice(p * tracks, (p + 1) * tracks)
            gene_ref[w, :, at] = gene_in[w * group + p, :capacity, :]
            loss_ref[w:w + 1, at] = loss_in[w * group + p, :1, :]

    if square:
        near_to(beside).wait_send()
        near_to(across).wait_send()
        pass_on(0, beside, across).wait_send()
        pass_on(1, across, beside).wait_send()
    else:
        for there in order:
            near_to(there).wait_send()
    for k in range(1, n_trk):
        sibling(k, x_hbm, place).wait_send()
        for frm in order:
            sibling(k, x_all.at[core, frm], frm).wait_send()


def round_up(n, m):
    return (n + m - 1) // m * m


def per_device(embeddings, head, exon_starts, exon_lengths, gene_owner, gene_targets):
    n_seq = lax.axis_size("seq")
    n_trk = lax.axis_size("trk")
    me = lax.axis_index("seq")
    windows, bin_dev, chans = embeddings.shape
    genes = gene_owner.shape[1]
    capacity = gene_targets.shape[1]
    group = n_seq // windows
    depth, track_dev = head.shape
    tracks = track_dev // group
    rows = windows * bin_dev
    own_rows = depth // n_seq
    row_pad = round_up(own_rows, 16)
    cap_pad = round_up(capacity, 8)
    bf16, f32 = jnp.bfloat16, jnp.float32

    head_parts = head.reshape(n_trk, chans, track_dev)
    if tracks % 128:
        head_parts = lax.dynamic_slice_in_dim(head_parts, me % group * tracks, tracks, 2)

    dma = pltpu.SemaphoreType.DMA
    vmem = pl.BlockSpec(memory_space=pltpu.VMEM)
    hbm = pl.BlockSpec(memory_space=pl.ANY)
    grad, gene, loss = pl.pallas_call(
        functools.partial(kernel, (n_seq, n_trk, windows, group, genes, own_rows)),
        out_shape=(
            jax.ShapeDtypeStruct((own_rows, track_dev), f32),
            jax.ShapeDtypeStruct((windows, capacity, track_dev), f32),
            jax.ShapeDtypeStruct((windows, track_dev), f32),
        ),
        in_specs=[hbm, hbm, vmem, vmem, vmem, vmem],
        out_specs=(vmem, vmem, vmem),
        scratch_shapes=[
            pltpu.VMEM((n_trk, group, rows, chans), bf16),
            pltpu.VMEM((n_trk, chans, tracks), bf16),
            pltpu.VMEM((group, windows * genes, rows), bf16),
            pltpu.VMEM((n_seq, cap_pad, tracks), f32),
            pltpu.VMEM((n_seq, cap_pad, tracks), f32),
            pltpu.VMEM((n_seq, 8, tracks), f32),
            pltpu.VMEM((rows, tracks), bf16),
            pltpu.VMEM((group, rows, tracks), f32),
            pltpu.VMEM((windows, genes, tracks), f32),
            pltpu.VMEM((windows, genes, tracks), f32),
            pltpu.VMEM((windows, genes, tracks), bf16),
            pltpu.VMEM((n_seq, cap_pad, tracks), f32),
            pltpu.VMEM((n_seq, cap_pad, tracks), f32),
            pltpu.VMEM((8, tracks), f32),
            pltpu.VMEM((group, rows, tracks), bf16),
            pltpu.VMEM((chans, tracks), f32),
            pltpu.VMEM((n_seq, row_pad, tracks), bf16),
            pltpu.VMEM((n_seq, row_pad, tracks), bf16),
            dma((group,)), dma((group,)),
            dma((n_trk, group)), dma((n_trk, group)),
            dma((n_seq,)), dma((n_seq,)),
            dma((windows,)), dma((windows,)),
            dma((windows,)), dma((windows,)),
            dma((n_seq,)), dma((n_seq,)),
            dma((n_seq,)), dma((n_seq,)),
            dma((n_seq,)), dma((n_seq,)),
            dma((2,)), dma((2,)), dma, dma,
        ],
        compiler_params=pltpu.CompilerParams(
            collective_id=0, has_side_effects=True, vmem_limit_bytes=60 * 1024 * 1024
        ),
    )(
        embeddings.reshape(rows, chans), head_parts, exon_starts, exon_lengths, gene_owner,
        gene_targets,
    )

    return gene, loss, grad


def solution(mesh):
    return jax.shard_map(
        per_device,
        mesh=mesh,
        in_specs=(P(None, "seq", "trk"), P(None, "trk"), P(), P(), P(), P(None, "seq", "trk")),
        out_specs=(P(None, "seq", "trk"), P(None, "trk"), P("seq", "trk")),
        check_vma=False,
    )
```

```python
import functools

import jax
import jax.numpy as jnp
from jax import lax
from jax.experimental import pallas as pl
from jax.experimental.pallas import tpu as pltpu
from jax.sharding import PartitionSpec as P

MESH = pl.DeviceIdType.MESH
HIGHEST = lax.Precision.HIGHEST


def kernel(
    dims,
    x_hbm, head_hbm, exons_ref, owner_ref, targets_ref,
    grad_ref, gene_ref, loss_ref,
    x_all, head_ref, mem_ref, tgt_ref, gene_in, loss_in, pred, sig, part, part_in, grads, tgt_in, gene_out, loss_out, lgrad, acc, block_out, block_in,
    near_send, near_recv, sib_send, sib_recv, tgt_send, tgt_recv, part_send, part_recv,
    grads_send, grads_recv, gene_send, gene_recv, loss_send, loss_recv, block_send, block_recv,
    diag_send, diag_recv, own_sem, head_sem, pair_in, pair_send, pair_recv,
):
    n_seq, n_trk, windows, group, genes, own_rows = dims
    me = lax.axis_index("seq")
    core = lax.axis_index("trk")
    win = me // group
    place = lax.rem(me, group)
    rows, chans = x_all.shape[2:]
    tracks = head_ref.shape[2]
    bin_dev = rows // windows
    capacity = targets_ref.shape[1]
    cap_pad = tgt_ref.shape[1]
    square = group == 4 and rows % 32 == 0
    tile = 256 if rows % 256 == 0 else rows

    def to_seq(src, dst, send, recv, there):
        return pltpu.make_async_remote_copy(
            src_ref=src, dst_ref=dst, send_sem=send, recv_sem=recv,
            device_id={"seq": there}, device_id_type=MESH,
        )

    def to_core(src, dst, send, recv, there):
        return pltpu.make_async_remote_copy(
            src_ref=src, dst_ref=dst, send_sem=send, recv_sem=recv,
            device_id={"trk": there}, device_id_type=MESH,
        )

    barrier = pltpu.get_barrier_semaphore()

    @pl.loop(1, n_seq)
    def _(k):
        pl.semaphore_signal(
            barrier, inc=1, device_id={"seq": lax.rem(me + k, n_seq)}, device_id_type=MESH
        )

    for k in range(1, n_trk):
        pl.semaphore_signal(
            barrier, inc=1, device_id={"trk": lax.rem(core + k, n_trk)}, device_id_type=MESH
        )
    pl.semaphore_wait(barrier, n_seq - 1 + n_trk - 1)

    def near_to(there):
        return to_seq(
            x_hbm, x_all.at[core, place], near_send.at[there], near_recv.at[place],
            win * group + there,
        )

    def near_from(frm):
        return to_seq(
            x_hbm, x_all.at[core, frm], near_send.at[frm], near_recv.at[frm], win * group + frm
        )

    def sibling(k, source, slot):
        there = lax.rem(core + k, n_trk)
        return to_core(
            source, x_all.at[core, slot], sib_send.at[there, slot], sib_recv.at[core, slot], there
        )

    def sibling_arrival(k, slot):
        frm = lax.rem(core + k, n_trk)
        return to_core(
            x_hbm, x_all.at[frm, slot], sib_send.at[frm, slot], sib_recv.at[frm, slot], frm
        )

    half = rows // 2
    beside = place + 1 - 2 * lax.rem(place, 2)
    across = lax.rem(place + 2, group)
    corner = group - 1 - place

    def pass_on(part_of, frm, there):
        at = x_all.at[core, frm, pl.ds(part_of * half, half)]
        return to_seq(
            at, at, diag_send.at[part_of], diag_recv.at[part_of], win * group + there
        )

    if square:
        order = [beside, across, corner]
        near_to(beside).start()
        near_to(across).start()
    else:
        order = [lax.rem(place + k, group) for k in range(1, group)]
        for there in order:
            near_to(there).start()
    for k in range(1, n_trk):
        sibling(k, x_hbm, place).start()
    own_copy = pltpu.make_async_copy(x_hbm, x_all.at[core, place], own_sem)
    own_copy.start()
    if head_hbm.shape[2] == tracks:
        head_copy = pltpu.make_async_copy(head_hbm, head_ref, head_sem)
    else:
        at = pl.ds(pl.multiple_of(place * tracks, tracks), tracks)
        head_copy = pltpu.make_async_copy(head_hbm.at[:, :, at], head_ref, head_sem)
    head_copy.start()

    def tgt_copy(k):
        there = lax.rem(me + k, n_seq)
        return to_seq(tgt_ref.at[there], tgt_in.at[me], tgt_send.at[there], tgt_recv.at[me], there)

    tgt_ref[...] = jnp.zeros_like(tgt_ref)
    for w in range(windows):
        for p in range(group):
            tgt_ref[w * group + p, :capacity, :] = (
                targets_ref[w, :, p * tracks:(p + 1) * tracks]
            )

    @pl.loop(1, n_seq)
    def _(k):
        tgt_copy(k).start()

    tgt_in[me] = tgt_ref[me]

    mem_ref[...] = jnp.zeros_like(mem_ref)
    exons = exons_ref.shape[2] // 2

    @pl.loop(0, group)
    def _(slot):
        bins = (win * group + slot) * bin_dev + lax.broadcasted_iota(
            jnp.int32, (genes, bin_dev), 1
        )
        for w in range(windows):
            table = exons_ref[w]
            count = jnp.zeros((genes, bin_dev), jnp.float32)
            for e in range(exons):
                begin = table[:, e:e + 1]
                end = begin + table[:, exons + e:exons + e + 1]
                count += jnp.where((bins >= begin) & (bins < end), 1.0, 0.0)
            mem_ref[slot, w * genes:(w + 1) * genes, w * bin_dev:(w + 1) * bin_dev] = (
                count.astype(jnp.bfloat16)
            )

    owner_row = owner_ref[pl.ds(win, 1), :]
    down = lax.broadcasted_iota(jnp.int32, (genes, genes), 0)
    along = lax.broadcasted_iota(jnp.int32, (genes, genes), 1)
    spread_row = jnp.broadcast_to(owner_row, (genes, genes))
    owner_col = jnp.sum(jnp.where(down == along, spread_row, 0), axis=1, keepdims=True)
    same = spread_row == owner_col
    rank_col = jnp.sum(jnp.where(same & (along < down), 1, 0), axis=1, keepdims=True)
    rank_row = jnp.sum(jnp.where(same & (down < along), 1, 0), axis=0, keepdims=True)
    slot_col = owner_col * cap_pad + rank_col
    slot_row = owner_row * cap_pad + rank_row
    slots = n_seq * cap_pad
    pick = jnp.where(
        slot_col == lax.broadcasted_iota(jnp.int32, (genes, slots), 1), 1.0, 0.0
    )
    give = jnp.where(
        slot_row == lax.broadcasted_iota(jnp.int32, (slots, genes), 0), 1.0, 0.0
    )

    part[...] = jnp.zeros_like(part)

    def forward(slot):
        @pl.loop(0, rows // tile)
        def _(i):
            at = pl.ds(pl.multiple_of(i * tile, tile), tile)
            logits = jnp.dot(
                x_all[0, slot, at, :], head_ref[0], preferred_element_type=jnp.float32
            )
            for c in range(1, n_trk):
                logits += jnp.dot(
                    x_all[c, slot, at, :], head_ref[c], preferred_element_type=jnp.float32
                )
            small = jnp.exp(-jnp.abs(logits))
            pred[at, :] = (jnp.maximum(logits, 0.0) + jnp.log1p(small)).astype(jnp.bfloat16)
            sig[slot, at, :] = jnp.where(logits >= 0, 1.0, small) / (1.0 + small)

        part[...] += jnp.dot(
            mem_ref[slot], pred[...], preferred_element_type=jnp.float32
        ).reshape(part.shape)

    own_copy.wait()
    head_copy.wait()

    def hand_over(frm):
        for j in range(1, n_trk):
            sibling(j, x_all.at[core, frm], frm).start()

    if square:
        near_from(beside).wait_recv()
        pass_on(0, beside, across).start()
        hand_over(beside)
        near_from(across).wait_recv()
        pass_on(1, across, beside).start()
        hand_over(across)
        ready = [place, beside, across]
    else:
        ready = [place]
    for slot in ready:
        for j in range(1, n_trk):
            sibling_arrival(j, slot).wait_recv()
        forward(slot)
    for frm in order[len(ready) - 1:]:
        if square:
            pass_on(0, frm, across).wait_recv()
            pass_on(1, frm, beside).wait_recv()
        else:
            near_from(frm).wait_recv()
        hand_over(frm)
        for j in range(1, n_trk):
            sibling_arrival(j, frm).wait_recv()
        forward(frm)

    def part_copy(k):
        there = lax.rem(win + k, windows)
        return to_seq(
            part.at[there], part_in.at[win], part_send.at[there], part_recv.at[win],
            there * group + place,
        )

    for k in range(1, windows):
        part_copy(k).start()

    @pl.loop(1, n_seq)
    def _(k):
        frm = lax.rem(me + k, n_seq)
        to_seq(
            tgt_ref.at[frm], tgt_in.at[frm], tgt_send.at[frm], tgt_recv.at[frm], frm
        ).wait_recv()

    tgt = jnp.dot(
        pick, tgt_in[...].reshape(-1, tracks),
        preferred_element_type=jnp.float32, precision=HIGHEST,
    )
    tsum = jnp.sum(tgt, axis=0, keepdims=True)
    part_in[win] = part[win]
    for k in range(1, windows):
        frm = lax.rem(win + k, windows)
        to_seq(
            part.at[frm], part_in.at[frm], part_send.at[frm], part_recv.at[frm],
            frm * group + place,
        ).wait_recv()
    gene = part_in[0]
    for k in range(1, windows):
        gene += part_in[k]
    total = jnp.sum(gene, axis=0, keepdims=True)
    grads[win] = (
        (genes / tsum) * ((0.2 + 0.8 * tsum / total) - tgt / gene)
    ).astype(jnp.bfloat16)

    def grads_copy(k):
        there = lax.rem(win + k, windows)
        return to_seq(
            grads.at[win], grads.at[win], grads_send.at[there], grads_recv.at[win],
            there * group + place,
        )

    for k in range(1, windows):
        grads_copy(k).start()

    fit = jnp.sum(tgt * jnp.log(gene), axis=0, keepdims=True)
    log_total = jnp.log(total)
    loss = (-fit + tsum * log_total + 0.2 * (total - tsum * log_total)) / tsum
    loss_out[...] = jnp.broadcast_to(loss, loss_out.shape)
    gene_out[...] = jnp.dot(
        give, gene, preferred_element_type=jnp.float32, precision=HIGHEST
    ).reshape(gene_out.shape)

    def gene_copy(k):
        there = lax.rem(me + k, n_seq)
        return to_seq(
            gene_out.at[there], gene_in.at[me], gene_send.at[there], gene_recv.at[me], there
        )

    def loss_copy(k):
        there = lax.rem(me + k, n_seq)
        return to_seq(loss_out, loss_in.at[me], loss_send.at[there], loss_recv.at[me], there)

    gene_in[me] = gene_out[me]
    loss_in[me] = loss_out[...]

    for k in range(1, windows):
        frm = lax.rem(win + k, windows)
        to_seq(
            grads.at[frm], grads.at[frm], grads_send.at[frm], grads_recv.at[frm],
            frm * group + place,
        ).wait_recv()

    @pl.loop(1, n_seq)
    def _(k):
        gene_copy(k).start()
        loss_copy(k).start()

    @pl.loop(0, group)
    def _(slot):
        spread = lax.dot_general(
            mem_ref[slot], grads[...].reshape(-1, tracks), (((0,), (0,)), ((), ())),
            preferred_element_type=jnp.float32,
        )
        lgrad[slot] = (spread * sig[slot]).astype(jnp.bfloat16)

    blocks = n_seq // n_trk

    def block_copy(there):
        return to_seq(
            block_out.at[there], block_in.at[me], block_send.at[there], block_recv.at[me], there
        )

    paired = windows == 4 and n_trk == 2
    partner = win + 1 - 2 * lax.rem(win, 2)
    opposite = lax.rem(win + 2, windows)

    def pair_copy():
        at = pl.ds(lax.rem(partner + 2, windows) * group, group)
        return to_seq(
            block_out.at[at], pair_in, pair_send, pair_recv, partner * group + place
        )

    for i in range(n_trk):
        c = lax.rem(2 * n_trk - 1 - win * n_trk // windows + i, n_trk)
        acc[...] = jnp.zeros_like(acc)

        @pl.loop(0, group)
        def _(slot):
            acc[...] += lax.dot_general(
                x_all[c, slot], lgrad[slot], (((0,), (0,)), ((), ())),
                preferred_element_type=jnp.float32,
            )

        for j in range(blocks):
            there = c * blocks + j
            value = acc[j * own_rows:(j + 1) * own_rows].astype(jnp.bfloat16)
            spare = block_out.shape[1] - own_rows
            if spare:
                value = jnp.concatenate([value, jnp.zeros((spare, tracks), jnp.bfloat16)], axis=0)
            block_out[there] = value

            if i > 0 or not paired:
                @pl.when(me != there)
                def _():
                    block_copy(there).start()

        if i == 0 and paired:
            pair_copy().start()

    block_in[me] = block_out[me]
    if paired:
        pair_copy().wait_recv()
        for p in range(group):
            there = opposite * group + p
            block_out[there] = (
                block_out[there].astype(jnp.float32) + pair_in[p].astype(jnp.float32)
            ).astype(jnp.bfloat16)
            block_copy(there).start()
        terms = [win, partner, opposite]
    else:
        terms = [lax.rem(win + k, windows) for k in range(windows)]

    def block_arrival(frm):
        return to_seq(
            block_out.at[frm], block_in.at[frm], block_send.at[frm], block_recv.at[frm], frm
        )

    for k in range(1, group):
        block_arrival(win * group + lax.rem(place + k, group)).wait_recv()
    for w in terms[1:]:
        for p in range(group):
            block_arrival(w * group + p).wait_recv()

    for p in range(group):
        whole = block_in[terms[0] * group + p].astype(jnp.float32)
        for w in terms[1:]:
            whole += block_in[w * group + p].astype(jnp.float32)
        grad_ref[:, p * tracks:(p + 1) * tracks] = whole[:own_rows]

    for k in range(1, group):
        block_copy(win * group + lax.rem(place + k, group)).wait_send()
    for w in terms[1:]:
        for p in range(group):
            block_copy(w * group + p).wait_send()
    if paired:
        pair_copy().wait_send()

    @pl.loop(1, n_seq)
    def _(k):
        frm = lax.rem(me + k, n_seq)
        to_seq(
            gene_out.at[frm], gene_in.at[frm], gene_send.at[frm], gene_recv.at[frm], frm
        ).wait_recv()
        to_seq(loss_out, loss_in.at[frm], loss_send.at[frm], loss_recv.at[frm], frm).wait_recv()
        tgt_copy(k).wait_send()
        gene_copy(k).wait_send()
        loss_copy(k).wait_send()

    for k in range(1, windows):
        part_copy(k).wait_send()
        grads_copy(k).wait_send()
    for w in range(windows):
        for p in range(group):
            at = slice(p * tracks, (p + 1) * tracks)
            gene_ref[w, :, at] = gene_in[w * group + p, :capacity, :]
            loss_ref[w:w + 1, at] = loss_in[w * group + p, :1, :]

    if square:
        near_to(beside).wait_send()
        near_to(across).wait_send()
        pass_on(0, beside, across).wait_send()
        pass_on(1, across, beside).wait_send()
    else:
        for there in order:
            near_to(there).wait_send()
    for k in range(1, n_trk):
        sibling(k, x_hbm, place).wait_send()
        for frm in order:
            sibling(k, x_all.at[core, frm], frm).wait_send()


def round_up(n, m):
    return (n + m - 1) // m * m


def per_device(embeddings, head, exon_starts, exon_lengths, gene_owner, gene_targets):
    n_seq = lax.axis_size("seq")
    n_trk = lax.axis_size("trk")
    me = lax.axis_index("seq")
    windows, bin_dev, chans = embeddings.shape
    genes = gene_owner.shape[1]
    capacity = gene_targets.shape[1]
    group = n_seq // windows
    depth, track_dev = head.shape
    tracks = track_dev // group
    rows = windows * bin_dev
    own_rows = depth // n_seq
    row_pad = round_up(own_rows, 16)
    cap_pad = round_up(capacity, 8)
    bf16, f32 = jnp.bfloat16, jnp.float32

    head_parts = head.reshape(n_trk, chans, track_dev)
    if tracks % 128:
        head_parts = lax.dynamic_slice_in_dim(head_parts, me % group * tracks, tracks, 2)

    dma = pltpu.SemaphoreType.DMA
    vmem = pl.BlockSpec(memory_space=pltpu.VMEM)
    hbm = pl.BlockSpec(memory_space=pl.ANY)
    grad, gene, loss = pl.pallas_call(
        functools.partial(kernel, (n_seq, n_trk, windows, group, genes, own_rows)),
        out_shape=(
            jax.ShapeDtypeStruct((own_rows, track_dev), f32),
            jax.ShapeDtypeStruct((windows, capacity, track_dev), f32),
            jax.ShapeDtypeStruct((windows, track_dev), f32),
        ),
        in_specs=[hbm, hbm, vmem, vmem, vmem],
        out_specs=(vmem, vmem, vmem),
        scratch_shapes=[
            pltpu.VMEM((n_trk, group, rows, chans), bf16),
            pltpu.VMEM((n_trk, chans, tracks), bf16),
            pltpu.VMEM((group, windows * genes, rows), bf16),
            pltpu.VMEM((n_seq, cap_pad, tracks), f32),
            pltpu.VMEM((n_seq, cap_pad, tracks), f32),
            pltpu.VMEM((n_seq, 8, tracks), f32),
            pltpu.VMEM((rows, tracks), bf16),
            pltpu.VMEM((group, rows, tracks), f32),
            pltpu.VMEM((windows, genes, tracks), f32),
            pltpu.VMEM((windows, genes, tracks), f32),
            pltpu.VMEM((windows, genes, tracks), bf16),
            pltpu.VMEM((n_seq, cap_pad, tracks), f32),
            pltpu.VMEM((n_seq, cap_pad, tracks), f32),
            pltpu.VMEM((8, tracks), f32),
            pltpu.VMEM((group, rows, tracks), bf16),
            pltpu.VMEM((chans, tracks), f32),
            pltpu.VMEM((n_seq, row_pad, tracks), bf16),
            pltpu.VMEM((n_seq, row_pad, tracks), bf16),
            dma((group,)), dma((group,)),
            dma((n_trk, group)), dma((n_trk, group)),
            dma((n_seq,)), dma((n_seq,)),
            dma((windows,)), dma((windows,)),
            dma((windows,)), dma((windows,)),
            dma((n_seq,)), dma((n_seq,)),
            dma((n_seq,)), dma((n_seq,)),
            dma((n_seq,)), dma((n_seq,)),
            dma((2,)), dma((2,)), dma, dma,
            pltpu.VMEM((group, row_pad, tracks), bf16), dma, dma,
        ],
        compiler_params=pltpu.CompilerParams(
            collective_id=0, has_side_effects=True, vmem_limit_bytes=60 * 1024 * 1024
        ),
    )(
        embeddings.reshape(rows, chans), head_parts,
        jnp.concatenate([exon_starts, exon_lengths], axis=2), gene_owner, gene_targets,
    )

    return gene, loss, grad


def solution(mesh):
    return jax.shard_map(
        per_device,
        mesh=mesh,
        in_specs=(P(None, "seq", "trk"), P(None, "trk"), P(), P(), P(), P(None, "seq", "trk")),
        out_specs=(P(None, "seq", "trk"), P(None, "trk"), P("seq", "trk")),
        check_vma=False,
    )
```

```python
import functools

import jax
import jax.numpy as jnp
from jax import lax
from jax.experimental import pallas as pl
from jax.experimental.pallas import tpu as pltpu
from jax.sharding import PartitionSpec as P

MESH = pl.DeviceIdType.MESH
HIGHEST = lax.Precision.HIGHEST


def kernel(
    dims,
    x_hbm, head_hbm, exons_ref, owner_ref, targets_ref,
    grad_ref, gene_ref, loss_ref,
    x_all, head_ref, mem_ref, tgt_ref, gene_in, loss_in, pred, sig, part, part_in, grads, tgt_in, gene_out, loss_out, lgrad, acc, block_out, block_in,
    near_send, near_recv, sib_send, sib_recv, tgt_send, tgt_recv, part_send, part_recv,
    grads_send, grads_recv, gene_send, gene_recv, loss_send, loss_recv, block_send, block_recv,
    diag_send, diag_recv, own_sem, head_sem, pair_in, pair_send, pair_recv,
):
    n_seq, n_trk, windows, group, genes, own_rows = dims
    me = lax.axis_index("seq")
    core = lax.axis_index("trk")
    win = me // group
    place = lax.rem(me, group)
    rows, chans = x_all.shape[2:]
    tracks = head_ref.shape[2]
    bin_dev = rows // windows
    capacity = targets_ref.shape[1]
    cap_pad = tgt_ref.shape[1]
    square = group == 4 and rows % 32 == 0
    tile = 256 if rows % 256 == 0 else rows

    def to_seq(src, dst, send, recv, there):
        return pltpu.make_async_remote_copy(
            src_ref=src, dst_ref=dst, send_sem=send, recv_sem=recv,
            device_id={"seq": there}, device_id_type=MESH,
        )

    def to_core(src, dst, send, recv, there):
        return pltpu.make_async_remote_copy(
            src_ref=src, dst_ref=dst, send_sem=send, recv_sem=recv,
            device_id={"trk": there}, device_id_type=MESH,
        )

    barrier = pltpu.get_barrier_semaphore()

    @pl.loop(1, n_seq)
    def _(k):
        pl.semaphore_signal(
            barrier, inc=1, device_id={"seq": lax.rem(me + k, n_seq)}, device_id_type=MESH
        )

    for k in range(1, n_trk):
        pl.semaphore_signal(
            barrier, inc=1, device_id={"trk": lax.rem(core + k, n_trk)}, device_id_type=MESH
        )
    pl.semaphore_wait(barrier, n_seq - 1 + n_trk - 1)

    def near_to(there):
        return to_seq(
            x_hbm, x_all.at[core, place], near_send.at[there], near_recv.at[place],
            win * group + there,
        )

    def near_from(frm):
        return to_seq(
            x_hbm, x_all.at[core, frm], near_send.at[frm], near_recv.at[frm], win * group + frm
        )

    def sibling(k, source, slot):
        there = lax.rem(core + k, n_trk)
        return to_core(
            source, x_all.at[core, slot], sib_send.at[there, slot], sib_recv.at[core, slot], there
        )

    def sibling_arrival(k, slot):
        frm = lax.rem(core + k, n_trk)
        return to_core(
            x_hbm, x_all.at[frm, slot], sib_send.at[frm, slot], sib_recv.at[frm, slot], frm
        )

    half = rows // 2
    beside = place + 1 - 2 * lax.rem(place, 2)
    across = lax.rem(place + 2, group)
    corner = group - 1 - place

    def pass_on(part_of, frm, there):
        at = x_all.at[core, frm, pl.ds(part_of * half, half)]
        return to_seq(
            at, at, diag_send.at[part_of], diag_recv.at[part_of], win * group + there
        )

    if square:
        order = [beside, across, corner]
        near_to(beside).start()
        near_to(across).start()
    else:
        order = [lax.rem(place + k, group) for k in range(1, group)]
        for there in order:
            near_to(there).start()
    for k in range(1, n_trk):
        sibling(k, x_hbm, place).start()
    own_copy = pltpu.make_async_copy(x_hbm, x_all.at[core, place], own_sem)
    own_copy.start()
    if head_hbm.shape[2] == tracks:
        head_copy = pltpu.make_async_copy(head_hbm, head_ref, head_sem)
    else:
        at = pl.ds(pl.multiple_of(place * tracks, tracks), tracks)
        head_copy = pltpu.make_async_copy(head_hbm.at[:, :, at], head_ref, head_sem)
    head_copy.start()

    def tgt_copy(k):
        there = lax.rem(me + k, n_seq)
        return to_seq(tgt_ref.at[there], tgt_in.at[me], tgt_send.at[there], tgt_recv.at[me], there)

    tgt_ref[...] = jnp.zeros_like(tgt_ref)
    for w in range(windows):
        for p in range(group):
            tgt_ref[w * group + p, :capacity, :] = (
                targets_ref[w, :, p * tracks:(p + 1) * tracks]
            )

    @pl.loop(1, n_seq)
    def _(k):
        tgt_copy(k).start()

    tgt_in[me] = tgt_ref[me]

    mem_ref[...] = jnp.zeros_like(mem_ref)
    exons = exons_ref.shape[2] // 2

    @pl.loop(0, group)
    def _(slot):
        bins = (win * group + slot) * bin_dev + lax.broadcasted_iota(
            jnp.int32, (genes, bin_dev), 1
        )
        for w in range(windows):
            table = exons_ref[w]
            count = jnp.zeros((genes, bin_dev), jnp.float32)
            for e in range(exons):
                begin = table[:, e:e + 1]
                end = begin + table[:, exons + e:exons + e + 1]
                count += jnp.where((bins >= begin) & (bins < end), 1.0, 0.0)
            mem_ref[slot, w * genes:(w + 1) * genes, w * bin_dev:(w + 1) * bin_dev] = (
                count.astype(jnp.bfloat16)
            )

    owner_row = owner_ref[pl.ds(win, 1), :]
    down = lax.broadcasted_iota(jnp.int32, (genes, genes), 0)
    along = lax.broadcasted_iota(jnp.int32, (genes, genes), 1)
    spread_row = jnp.broadcast_to(owner_row, (genes, genes))
    owner_col = jnp.sum(jnp.where(down == along, spread_row, 0), axis=1, keepdims=True)
    same = spread_row == owner_col
    rank_col = jnp.sum(jnp.where(same & (along < down), 1, 0), axis=1, keepdims=True)
    rank_row = jnp.sum(jnp.where(same & (down < along), 1, 0), axis=0, keepdims=True)
    slot_col = owner_col * cap_pad + rank_col
    slot_row = owner_row * cap_pad + rank_row
    slots = n_seq * cap_pad
    pick = jnp.where(
        slot_col == lax.broadcasted_iota(jnp.int32, (genes, slots), 1), 1.0, 0.0
    )
    give = jnp.where(
        slot_row == lax.broadcasted_iota(jnp.int32, (slots, genes), 0), 1.0, 0.0
    )

    part[...] = jnp.zeros_like(part)

    def forward(slot):
        @pl.loop(0, rows // tile)
        def _(i):
            at = pl.ds(pl.multiple_of(i * tile, tile), tile)
            logits = jnp.dot(
                x_all[0, slot, at, :], head_ref[0], preferred_element_type=jnp.float32
            )
            for c in range(1, n_trk):
                logits += jnp.dot(
                    x_all[c, slot, at, :], head_ref[c], preferred_element_type=jnp.float32
                )
            small = jnp.exp(-jnp.abs(logits))
            pred[at, :] = (jnp.maximum(logits, 0.0) + jnp.log1p(small)).astype(jnp.bfloat16)
            sig[slot, at, :] = jnp.where(logits >= 0, 1.0, small) / (1.0 + small)

        part[...] += jnp.dot(
            mem_ref[slot], pred[...], preferred_element_type=jnp.float32
        ).reshape(part.shape)

    own_copy.wait()
    head_copy.wait()

    def hand_over(frm):
        for j in range(1, n_trk):
            sibling(j, x_all.at[core, frm], frm).start()

    if square:
        near_from(beside).wait_recv()
        pass_on(0, beside, across).start()
        hand_over(beside)
        near_from(across).wait_recv()
        pass_on(1, across, beside).start()
        hand_over(across)
        ready = [place, beside, across]
    else:
        ready = [place]
    for slot in ready:
        for j in range(1, n_trk):
            sibling_arrival(j, slot).wait_recv()
        forward(slot)
    for frm in order[len(ready) - 1:]:
        if square:
            pass_on(0, frm, across).wait_recv()
            pass_on(1, frm, beside).wait_recv()
        else:
            near_from(frm).wait_recv()
        hand_over(frm)
        for j in range(1, n_trk):
            sibling_arrival(j, frm).wait_recv()
        forward(frm)

    def part_copy(k):
        there = lax.rem(win + k, windows)
        return to_seq(
            part.at[there], part_in.at[win], part_send.at[there], part_recv.at[win],
            there * group + place,
        )

    for k in range(1, windows):
        part_copy(k).start()

    @pl.loop(1, n_seq)
    def _(k):
        frm = lax.rem(me + k, n_seq)
        to_seq(
            tgt_ref.at[frm], tgt_in.at[frm], tgt_send.at[frm], tgt_recv.at[frm], frm
        ).wait_recv()

    tgt = jnp.dot(
        pick, tgt_in[...].reshape(-1, tracks),
        preferred_element_type=jnp.float32, precision=HIGHEST,
    )
    tsum = jnp.sum(tgt, axis=0, keepdims=True)
    part_in[win] = part[win]
    for k in range(1, windows):
        frm = lax.rem(win + k, windows)
        to_seq(
            part.at[frm], part_in.at[frm], part_send.at[frm], part_recv.at[frm],
            frm * group + place,
        ).wait_recv()
    gene = part_in[0]
    for k in range(1, windows):
        gene += part_in[k]
    total = jnp.sum(gene, axis=0, keepdims=True)
    grads[win] = (
        (genes / tsum) * ((0.2 + 0.8 * tsum / total) - tgt / gene)
    ).astype(jnp.bfloat16)

    def grads_copy(k):
        there = lax.rem(win + k, windows)
        return to_seq(
            grads.at[win], grads.at[win], grads_send.at[there], grads_recv.at[win],
            there * group + place,
        )

    for k in range(1, windows):
        grads_copy(k).start()

    fit = jnp.sum(tgt * jnp.log(gene), axis=0, keepdims=True)
    log_total = jnp.log(total)
    loss = (-fit + tsum * log_total + 0.2 * (total - tsum * log_total)) / tsum
    loss_out[...] = jnp.broadcast_to(loss, loss_out.shape)
    gene_out[...] = jnp.dot(
        give, gene, preferred_element_type=jnp.float32, precision=HIGHEST
    ).reshape(gene_out.shape)

    def gene_copy(k):
        there = lax.rem(me + k, n_seq)
        return to_seq(
            gene_out.at[there], gene_in.at[me], gene_send.at[there], gene_recv.at[me], there
        )

    def loss_copy(k):
        there = lax.rem(me + k, n_seq)
        return to_seq(loss_out, loss_in.at[me], loss_send.at[there], loss_recv.at[me], there)

    gene_in[me] = gene_out[me]
    loss_in[me] = loss_out[...]

    for k in range(1, windows):
        frm = lax.rem(win + k, windows)
        to_seq(
            grads.at[frm], grads.at[frm], grads_send.at[frm], grads_recv.at[frm],
            frm * group + place,
        ).wait_recv()

    @pl.loop(1, n_seq)
    def _(k):
        gene_copy(k).start()
        loss_copy(k).start()

    @pl.loop(0, group)
    def _(slot):
        spread = lax.dot_general(
            mem_ref[slot], grads[...].reshape(-1, tracks), (((0,), (0,)), ((), ())),
            preferred_element_type=jnp.float32,
        )
        lgrad[slot] = (spread * sig[slot]).astype(jnp.bfloat16)

    blocks = n_seq // n_trk

    def block_copy(there):
        return to_seq(
            block_out.at[there], block_in.at[me], block_send.at[there], block_recv.at[me], there
        )

    paired = windows == 4 and n_trk == 2
    partner = win + 1 - 2 * lax.rem(win, 2)
    opposite = lax.rem(win + 2, windows)

    def pair_copy(p):
        there = lax.rem(partner + 2, windows) * group + p
        return to_seq(
            block_out.at[there], pair_in.at[p], pair_send.at[p], pair_recv.at[p],
            partner * group + place,
        )

    for i in range(n_trk):
        c = lax.rem(2 * n_trk - 1 - win * n_trk // windows + i, n_trk)
        acc[...] = jnp.zeros_like(acc)

        @pl.loop(0, group)
        def _(slot):
            acc[...] += lax.dot_general(
                x_all[c, slot], lgrad[slot], (((0,), (0,)), ((), ())),
                preferred_element_type=jnp.float32,
            )

        for j in range(blocks):
            there = c * blocks + j
            value = acc[j * own_rows:(j + 1) * own_rows].astype(jnp.bfloat16)
            spare = block_out.shape[1] - own_rows
            if spare:
                value = jnp.concatenate([value, jnp.zeros((spare, tracks), jnp.bfloat16)], axis=0)
            block_out[there] = value

            if i > 0 or not paired:
                @pl.when(me != there)
                def _():
                    block_copy(there).start()

        if i == 0 and paired:
            for p in range(group):
                pair_copy(p).start()

    block_in[me] = block_out[me]
    if paired:
        for p in range(group):
            pair_copy(p).wait_recv()
            there = opposite * group + p
            block_out[there] = (
                block_out[there].astype(jnp.float32) + pair_in[p].astype(jnp.float32)
            ).astype(jnp.bfloat16)
            block_copy(there).start()
        terms = [win, partner, opposite]
    else:
        terms = [lax.rem(win + k, windows) for k in range(windows)]

    def block_arrival(frm):
        return to_seq(
            block_out.at[frm], block_in.at[frm], block_send.at[frm], block_recv.at[frm], frm
        )

    for k in range(1, group):
        block_arrival(win * group + lax.rem(place + k, group)).wait_recv()
    for w in terms[1:]:
        for p in range(group):
            block_arrival(w * group + p).wait_recv()

    for p in range(group):
        whole = block_in[terms[0] * group + p].astype(jnp.float32)
        for w in terms[1:]:
            whole += block_in[w * group + p].astype(jnp.float32)
        grad_ref[:, p * tracks:(p + 1) * tracks] = whole[:own_rows]

    for k in range(1, group):
        block_copy(win * group + lax.rem(place + k, group)).wait_send()
    for w in terms[1:]:
        for p in range(group):
            block_copy(w * group + p).wait_send()
    if paired:
        for p in range(group):
            pair_copy(p).wait_send()

    @pl.loop(1, n_seq)
    def _(k):
        frm = lax.rem(me + k, n_seq)
        to_seq(
            gene_out.at[frm], gene_in.at[frm], gene_send.at[frm], gene_recv.at[frm], frm
        ).wait_recv()
        to_seq(loss_out, loss_in.at[frm], loss_send.at[frm], loss_recv.at[frm], frm).wait_recv()
        tgt_copy(k).wait_send()
        gene_copy(k).wait_send()
        loss_copy(k).wait_send()

    for k in range(1, windows):
        part_copy(k).wait_send()
        grads_copy(k).wait_send()
    for w in range(windows):
        for p in range(group):
            at = slice(p * tracks, (p + 1) * tracks)
            gene_ref[w, :, at] = gene_in[w * group + p, :capacity, :]
            loss_ref[w:w + 1, at] = loss_in[w * group + p, :1, :]

    if square:
        near_to(beside).wait_send()
        near_to(across).wait_send()
        pass_on(0, beside, across).wait_send()
        pass_on(1, across, beside).wait_send()
    else:
        for there in order:
            near_to(there).wait_send()
    for k in range(1, n_trk):
        sibling(k, x_hbm, place).wait_send()
        for frm in order:
            sibling(k, x_all.at[core, frm], frm).wait_send()


def round_up(n, m):
    return (n + m - 1) // m * m


def per_device(embeddings, head, exon_starts, exon_lengths, gene_owner, gene_targets):
    n_seq = lax.axis_size("seq")
    n_trk = lax.axis_size("trk")
    me = lax.axis_index("seq")
    windows, bin_dev, chans = embeddings.shape
    genes = gene_owner.shape[1]
    capacity = gene_targets.shape[1]
    group = n_seq // windows
    depth, track_dev = head.shape
    tracks = track_dev // group
    rows = windows * bin_dev
    own_rows = depth // n_seq
    row_pad = round_up(own_rows, 16)
    cap_pad = round_up(capacity, 8)
    bf16, f32 = jnp.bfloat16, jnp.float32

    head_parts = head.reshape(n_trk, chans, track_dev)
    if tracks % 128:
        head_parts = lax.dynamic_slice_in_dim(head_parts, me % group * tracks, tracks, 2)

    dma = pltpu.SemaphoreType.DMA
    vmem = pl.BlockSpec(memory_space=pltpu.VMEM)
    hbm = pl.BlockSpec(memory_space=pl.ANY)
    grad, gene, loss = pl.pallas_call(
        functools.partial(kernel, (n_seq, n_trk, windows, group, genes, own_rows)),
        out_shape=(
            jax.ShapeDtypeStruct((own_rows, track_dev), f32),
            jax.ShapeDtypeStruct((windows, capacity, track_dev), f32),
            jax.ShapeDtypeStruct((windows, track_dev), f32),
        ),
        in_specs=[hbm, hbm, vmem, vmem, vmem],
        out_specs=(vmem, vmem, vmem),
        scratch_shapes=[
            pltpu.VMEM((n_trk, group, rows, chans), bf16),
            pltpu.VMEM((n_trk, chans, tracks), bf16),
            pltpu.VMEM((group, windows * genes, rows), bf16),
            pltpu.VMEM((n_seq, cap_pad, tracks), f32),
            pltpu.VMEM((n_seq, cap_pad, tracks), f32),
            pltpu.VMEM((n_seq, 8, tracks), f32),
            pltpu.VMEM((rows, tracks), bf16),
            pltpu.VMEM((group, rows, tracks), f32),
            pltpu.VMEM((windows, genes, tracks), f32),
            pltpu.VMEM((windows, genes, tracks), f32),
            pltpu.VMEM((windows, genes, tracks), bf16),
            pltpu.VMEM((n_seq, cap_pad, tracks), f32),
            pltpu.VMEM((n_seq, cap_pad, tracks), f32),
            pltpu.VMEM((8, tracks), f32),
            pltpu.VMEM((group, rows, tracks), bf16),
            pltpu.VMEM((chans, tracks), f32),
            pltpu.VMEM((n_seq, row_pad, tracks), bf16),
            pltpu.VMEM((n_seq, row_pad, tracks), bf16),
            dma((group,)), dma((group,)),
            dma((n_trk, group)), dma((n_trk, group)),
            dma((n_seq,)), dma((n_seq,)),
            dma((windows,)), dma((windows,)),
            dma((windows,)), dma((windows,)),
            dma((n_seq,)), dma((n_seq,)),
            dma((n_seq,)), dma((n_seq,)),
            dma((n_seq,)), dma((n_seq,)),
            dma((2,)), dma((2,)), dma, dma,
            pltpu.VMEM((group, row_pad, tracks), bf16), dma((group,)), dma((group,)),
        ],
        compiler_params=pltpu.CompilerParams(
            collective_id=0, has_side_effects=True, vmem_limit_bytes=60 * 1024 * 1024
        ),
    )(
        embeddings.reshape(rows, chans), head_parts,
        jnp.concatenate([exon_starts, exon_lengths], axis=2), gene_owner, gene_targets,
    )

    return gene, loss, grad


def solution(mesh):
    return jax.shard_map(
        per_device,
        mesh=mesh,
        in_specs=(P(None, "seq", "trk"), P(None, "trk"), P(), P(), P(), P(None, "seq", "trk")),
        out_specs=(P(None, "seq", "trk"), P(None, "trk"), P("seq", "trk")),
        check_vma=False,
    )
```
